256 devices in a mesh: outer: 4 (over y_lo, core), atoms: 64 (over z, x, y_hi).
Axes of the slice: x: 4, y: 4 (y_hi: 2, y_lo: 2; y = y_hi * 2 + y_lo), z: 8, core: 2. Of those that a mesh axis runs over, the one named last changes fastest.
Arguments:
- features: float32 [262144, 128], P(('outer', 'atoms')), may hold values from -6 to 6
- positions: int32 [3, 262144], P(None, ('outer', 'atoms')), may hold values from 0 to 262143
- wavevectors: int32 [3, 768], replicated, may hold values from -6 to 6
- w_value: float32 [2, 128, 128], replicated, may hold values from -0.5 to 0.5
- freq_filter: float32 [2, 768, 128], replicated, may hold values from 0.05 to 1
- norm_gain: float32 [2, 128], replicated, may hold values from 0.1 to 1.9
- w_hidden: float32 [2, 128, 128], replicated, may hold values from -0.5 to 0.5
- b_hidden: float32 [2, 128], replicated, may hold values from -4 to 4
- w_output: float32 [2, 128, 128], replicated, may hold values from -0.5 to 0.5
Outputs:
- updated: float32 [262144, 128], P(('outer', 'atoms'))
The draws below stay inside these ranges and needn't reach their ends.
All inputs are finite; a program needn't handle non-finite values.
Results may differ from the reference program's by a relative error of at most 0.0003.
Values sent between devices are 32-bit elements; how exact they have to be, the bound alone decides.
A program may use at most 64 MiB of HBM per device.

```python
import math
import jax
import jax.numpy as jnp
from jax import lax

ATOM_DEV = 1024
CHANNELS = 128
WAVES = 768
BLOCKS = 2
ATOMS = 262144


def place_ends(result, own_key, low, largest):
    shape = result.shape
    index_at = [jax.random.randint(jax.random.fold_in(own_key, axis), (), 0, shape[axis]) for axis in range(len(shape))]
    result = result.at[tuple(index_at)].set(low)
    longest = shape.index(max(shape))
    index_at[longest] = (index_at[longest] + 1) % shape[longest]
    return result.at[tuple(index_at)].set(largest)


def steps_of(own_key, extent, cuts, smallest, high):
    level, own = 1.0, jax.random.fold_in(own_key, 6)
    for axis_at, shards_of in cuts:
        draws = jnp.exp(jax.random.uniform(jax.random.fold_in(own, axis_at), (shards_of,), jnp.float32, smallest / len(cuts), high / len(cuts)))
        level = level * jnp.repeat(draws, extent[axis_at] // shards_of).reshape([-1 if axis == axis_at else 1 for axis in range(len(extent))])
    return level


def normal_values(rng, extent, deviation, most, pieces=(), held_as=jnp.bfloat16):
    drawn = deviation * jax.random.normal(rng, extent, jnp.float32)
    if pieces:
        drawn = drawn * steps_of(rng, extent, pieces, -0.22, 0.18)
    return jnp.clip(drawn, -most, most).astype(held_as)


def setup_inputs(seed: int = 0) -> dict:
    arg_keys = jax.random.split(jax.random.key(seed), 10)
    return {
        "features": normal_values(arg_keys[0], (ATOMS, CHANNELS), 1.0, 6.0, ((0, 256),), jnp.float32),
        "positions": place_ends(jax.random.randint(arg_keys[1], (3, ATOMS), 0, 262144), jax.random.fold_in(arg_keys[1], 1), 0, 262143).astype(jnp.int32),
        "wavevectors": place_ends(jax.random.randint(arg_keys[2], (3, WAVES), -6, 7), jax.random.fold_in(arg_keys[2], 1), -6, 6).astype(jnp.int32),
        "w_value": normal_values(arg_keys[3], (BLOCKS, CHANNELS, CHANNELS), CHANNELS ** -0.5, 0.5, (), jnp.float32),
        "freq_filter": jnp.clip(jnp.exp(jax.random.uniform(arg_keys[4], (BLOCKS, WAVES, CHANNELS), jnp.float32, math.log(0.05), math.log(1.0))), 0.05, 1.0),
        "norm_gain": jnp.clip(1.0 + 0.18 * jax.random.normal(arg_keys[5], (BLOCKS, CHANNELS), jnp.float32), 0.1, 1.9),
        "w_hidden": normal_values(arg_keys[6], (BLOCKS, CHANNELS, CHANNELS), CHANNELS ** -0.5, 0.5, (), jnp.float32),
        "b_hidden": normal_values(arg_keys[7], (BLOCKS, CHANNELS), 1.0, 4.0, (), jnp.float32),
        "w_output": normal_values(arg_keys[8], (BLOCKS, CHANNELS, CHANNELS), CHANNELS ** -0.5, 0.5, (), jnp.float32),
    }


fixed_scale = 262144
highest = lax.Precision.HIGHEST

def phases(pos_block, wave_block):
    integer_dot = pos_block[0][:, None] * wave_block[0][None, :]
    integer_dot = integer_dot + pos_block[1][:, None] * wave_block[1][None, :]
    integer_dot = integer_dot + pos_block[2][:, None] * wave_block[2][None, :]
    wrapped = jnp.mod(integer_dot, fixed_scale).astype(jnp.int32)
    return wrapped.astype(jnp.float32) * (2.0 * math.pi / fixed_scale)

def reference(features, positions, wavevectors, w_value, freq_filter, norm_gain, w_hidden, b_hidden, w_output):
    current = features
    pos_blocks = positions.reshape(3, -1, ATOM_DEV).transpose(1, 0, 2)
    for layer_index in range(BLOCKS):
        projected = jnp.dot(current, w_value[layer_index], precision=highest, preferred_element_type=jnp.float32)
        value_blocks = projected.reshape(-1, ATOM_DEV, CHANNELS)

        def accumulate(running, block_item):
            pos_block, value_block = block_item
            angles = phases(pos_block, wavevectors)
            real_part = jnp.einsum('ak,ac->kc', jnp.cos(angles), value_block, precision=highest)
            imag_part = -jnp.einsum('ak,ac->kc', jnp.sin(angles), value_block, precision=highest)
            return (running + jnp.concatenate([real_part, imag_part], axis=1), None)
        factor, _ = lax.scan(accumulate, jnp.zeros((WAVES, 2 * CHANNELS), jnp.float32), (pos_blocks, value_blocks))
        filtered = factor * jnp.concatenate([freq_filter[layer_index], freq_filter[layer_index]], axis=1)

        def back_project(pos_block):
            angles = phases(pos_block, wavevectors)
            first = jnp.dot(jnp.cos(angles), filtered[:, :CHANNELS], precision=highest, preferred_element_type=jnp.float32)
            second = jnp.dot(jnp.sin(angles), filtered[:, CHANNELS:], precision=highest, preferred_element_type=jnp.float32)
            return first - second
        messages = lax.map(back_project, pos_blocks).reshape(-1, CHANNELS)
        normed = messages * lax.rsqrt(lax.optimization_barrier(jnp.mean(messages * messages, axis=1, keepdims=True)) + 1e-06) * norm_gain[layer_index]
        hidden = jax.nn.silu(jnp.dot(normed, w_hidden[layer_index], precision=highest, preferred_element_type=jnp.float32) + b_hidden[layer_index])
        current = current + jnp.dot(hidden, w_output[layer_index], precision=highest, preferred_element_type=jnp.float32)
    return current
```

```python
import functools

import jax
import jax.numpy as jnp
from jax import lax
from jax.experimental import pallas as pl
from jax.experimental.pallas import tpu as pltpu
from jax.sharding import PartitionSpec as P

MESH = pl.DeviceIdType.MESH
f32 = jnp.float32
bf16 = jnp.bfloat16

NX, NY, NZ = 4, 4, 8
PLANE = NX * NY
ATOMS, CHANNELS, WAVES, BLOCKS = 1024, 128, 768, 2
ROWS = 2 * WAVES
HALF = ROWS // 2
CHUNKS = 3
CHUNK = HALF // CHUNKS
PIECE = CHUNK // PLANE
TURN = 262144.0

SIN = (
    6.283182818555351, -41.341421399021826, 81.59618388022938,
    -76.58010058938454, 41.20539511033188, -12.271262697277013,
)
COS = (
    0.999999989172279, -19.73920453209469, 64.93911898390982, -85.45016555036607,
    60.16783173144847, -25.968313301691698, 6.529610414314128,
)


def horner(coefficients, u):
    total = jnp.full_like(u, coefficients[-1])
    for c in coefficients[-2::-1]:
        total = total * u + c
    return total


def split(value):
    high = value.astype(bf16)
    return high, (value - high.astype(f32)).astype(bf16)


def dot(a, b):
    return jnp.dot(a, b, preferred_element_type=f32)


def dot_nt(a, b):
    return lax.dot_general(a, b, (((1,), (1,)), ((), ())), preferred_element_type=f32)


def hops(delta, size):
    return min(delta, size - delta)


PLANE_PEERS = sorted(
    ((dx, dy) for dx in range(NX) for dy in range(NY) if dx or dy),
    key=lambda d: -(hops(d[0], NX) + hops(d[1], NY)),
)
Z_PEERS = sorted(range(1, NZ), key=lambda d: -hops(d, NZ))


def body(
    feat_ref, pos_ref, wave_ref, wv_ref, filt_ref, gain_ref, wh_ref, bh_ref, wo_ref,
    out_ref,
    xs_ref, ws_ref, turn_ref, high_ref, low_ref, cur_ref, proj_ref, wvt_ref, wht_ref, wot_ref, bht_ref,
    away_ref, home_ref, cross_ref, plane_ref, mine_ref, depth_ref, fact_ref, acc_ref,
    cross_send, cross_recv, plane_send, plane_recv, depth_send, depth_recv,
    spread_send, spread_recv, pair_send, pair_recv,
    *, comm,
):
    outer, atoms = lax.axis_index("outer"), lax.axis_index("atoms")
    core, y = outer % 2, (atoms % 2) * 2 + outer // 2
    x, z = (atoms // 2) % NX, atoms // (2 * NX)
    me = x * NY + y

    def device(x, y, z, core):
        return ((y % 2) * 2 + core, z * (2 * NX) + x * 2 + y // 2)

    def plane_peer(delta):
        px, py = (x + delta[0]) % NX, (y + delta[1]) % NY
        return px * NY + py, device(px, py, z, core)

    other_core = device(x, y, z, 1 - core)

    def z_peer(delta):
        return device(x, y, (z + delta) % NZ, core)

    def send(source, target, send_sem, recv_sem, to):
        if comm:
            pltpu.make_async_remote_copy(
                src_ref=source, dst_ref=target, send_sem=send_sem, recv_sem=recv_sem,
                device_id=to, device_id_type=MESH,
            ).start()

    def wait(like, sem):
        if comm:
            pltpu.make_async_copy(like, like, sem).wait()

    if comm:
        barrier = pltpu.get_barrier_semaphore()
        for delta in PLANE_PEERS:
            pl.semaphore_signal(barrier, 1, device_id=plane_peer(delta)[1], device_id_type=MESH)
        for delta in Z_PEERS:
            pl.semaphore_signal(barrier, 1, device_id=z_peer(delta), device_id_type=MESH)
        pl.semaphore_signal(barrier, 1, device_id=other_core, device_id_type=MESH)

    positions = pos_ref[...]
    waves = wave_ref[...].astype(f32)
    xs_ref[...] = jnp.zeros_like(xs_ref)
    ws_ref[...] = jnp.zeros_like(ws_ref)
    for i in range(3):
        xs_ref[3 * i : 3 * i + 3, :] = ((positions >> (8 * i)) & 255).astype(f32)
        ws_ref[3 * i : 3 * i + 3, :] = waves * (256.0**i / TURN)
    turn_ref[...] = dot(ws_ref[...].T.astype(bf16), xs_ref[...].astype(bf16))

    for b in range(BLOCKS):
        for matrix, held in ((wv_ref[b], wvt_ref), (wh_ref[b] * gain_ref[b : b + 1, :].T, wht_ref), (wo_ref[b], wot_ref)):
            high, low = split(matrix.T)
            held[b, :CHANNELS, :] = high
            held[b, CHANNELS:, :] = low
        bht_ref[b] = jnp.broadcast_to(bh_ref[b : b + 1, :], (CHANNELS, CHANNELS)).T
    cur_ref[...] = feat_ref[...].T

    def weighted(held, b, value):
        high, low = split(value)
        both = dot(held[b], high)
        return both[:CHANNELS] + both[CHANNELS:] + dot(held[b, :CHANNELS, :], low)

    def project(b):
        high, low = split(weighted(wvt_ref, b, cur_ref[...]))
        proj_ref[:CHANNELS, :] = high
        proj_ref[CHANNELS:, :] = low

    def table(first_octet, count):
        def step(i, _):
            octet = first_octet + i
            t = turn_ref[pl.ds(pl.multiple_of(octet * 8, 8), 8), :]
            r = t - jnp.round(t)
            u = r * r
            pair = jnp.concatenate([horner(COS, u), horner(SIN, u) * r], axis=0)
            high, low = split(pair)
            at = pl.ds(pl.multiple_of(octet * 16, 16), 16)
            high_ref[at, :] = high
            low_ref[at, :] = low
            return 0

        lax.fori_loop(0, count, step, 0)

    project(0)
    for b in range(BLOCKS):
        for which in range(2):
            half = 1 - core if which == 0 else core
            for q in range(CHUNKS):
                chunk = half * CHUNKS + q
                if b == 0:
                    table(chunk * (CHUNK // 16), CHUNK // 16)
                rows = pl.ds(pl.multiple_of(chunk * CHUNK, CHUNK), CHUNK)
                both = dot_nt(high_ref[rows, :], proj_ref[...]) + dot_nt(low_ref[rows, :], proj_ref[...])
                part = both[:, :CHANNELS] + both[:, CHANNELS:]
                if which == 0:
                    away_ref[b, q] = part
                    if comm and b == 0 and q == 0:
                        pl.semaphore_wait(barrier, len(PLANE_PEERS) + len(Z_PEERS) + 1)
                    send(away_ref.at[b, q], cross_ref.at[b, q], cross_send.at[b, q], cross_recv.at[b, q], other_core)
                else:
                    wait(cross_ref.at[b, q], cross_recv.at[b, q])
                    home_ref[b, q] = part + cross_ref[b, q]
                    for delta in PLANE_PEERS:
                        peer, to = plane_peer(delta)
                        send(
                            home_ref.at[b, q, pl.ds(pl.multiple_of(peer * PIECE, 8), PIECE)],
                            plane_ref.at[b, q, me], plane_send.at[b, q], plane_recv.at[b, q], to,
                        )
                    plane_ref[b, q, me] = home_ref[b, q, pl.ds(pl.multiple_of(me * PIECE, 8), PIECE)]
        for q in range(CHUNKS):
            wait(plane_ref.at[b, q, pl.ds(0, PLANE - 1)], plane_recv.at[b, q])
            mine_ref[b, q] = jnp.sum(plane_ref[b, q], axis=0)
            for delta in Z_PEERS:
                send(mine_ref.at[b, q], depth_ref.at[b, q, z], depth_send.at[b, q], depth_recv.at[b, q], z_peer(delta))
            depth_ref[b, q, z] = mine_ref[b, q]
        for q in range(CHUNKS):
            wait(depth_ref.at[b, q, pl.ds(0, NZ - 1)], depth_recv.at[b, q])
            total = jnp.sum(depth_ref[b, q], axis=0)
            first = (core * CHUNKS + q) * CHUNK + me * PIECE
            parts = []
            for i in range(PIECE // 8):
                octet = (first // 8 + i) // 2
                parts.append(filt_ref[b, pl.ds(pl.multiple_of(octet * 8, 8), 8), :])
            here = fact_ref.at[b, pl.ds(pl.multiple_of(first, 8), PIECE)]
            here[...] = total * jnp.concatenate(parts, axis=0)
            for delta in PLANE_PEERS:
                send(here, here, spread_send.at[b, q], spread_recv.at[b, q], plane_peer(delta)[1])
        for q in range(CHUNKS):
            chunk = pl.ds(pl.multiple_of((core * CHUNKS + q) * CHUNK, CHUNK), CHUNK)
            wait(fact_ref.at[b, pl.ds(0, (PLANE - 1) * PIECE)], spread_recv.at[b, q])
            whole = fact_ref.at[b, chunk]
            send(whole, whole, pair_send.at[b, q], pair_recv.at[b, q], other_core)
        for which in range(2):
            half = core if which == 0 else 1 - core
            if which == 1:
                for q in range(CHUNKS):
                    wait(fact_ref.at[b, pl.ds(0, CHUNK)], pair_recv.at[b, q])
            rows = pl.ds(pl.multiple_of(half * HALF, HALF), HALF)
            high, low = split(fact_ref[b, rows, :].T)
            both = dot(jnp.concatenate([high, low], axis=0), high_ref[rows, :])
            part = both[:CHANNELS] + both[CHANNELS:] + dot(high, low_ref[rows, :])
            if which == 0:
                acc_ref[...] = part
            else:
                acc_ref[...] += part
        messages = acc_ref[...]
        scale = lax.rsqrt(jnp.mean(messages * messages, axis=0, keepdims=True) + 1e-6)
        bias = jnp.concatenate([bht_ref[b]] * (ATOMS // CHANNELS), axis=1)
        v = weighted(wht_ref, b, messages) * scale + bias
        hidden = v / (1.0 + jnp.exp(-v))
        cur_ref[...] += weighted(wot_ref, b, hidden)
        if b + 1 < BLOCKS:
            project(b + 1)
    out_ref[...] = cur_ref[...].T
    for b in range(BLOCKS):
        for q in range(CHUNKS):
            wait(away_ref.at[b, q], cross_send.at[b, q])
            wait(plane_ref.at[b, q, pl.ds(0, PLANE - 1)], plane_send.at[b, q])
            wait(depth_ref.at[b, q, pl.ds(0, NZ - 1)], depth_send.at[b, q])
            wait(fact_ref.at[b, pl.ds(0, (PLANE - 1) * PIECE)], spread_send.at[b, q])
            wait(fact_ref.at[b, pl.ds(0, CHUNK)], pair_send.at[b, q])


def local(*operands, comm=True):
    sems = [pltpu.SemaphoreType.DMA((BLOCKS, CHUNKS))] * 10
    return pl.pallas_call(
        functools.partial(body, comm=comm),
        name="ewald",
        out_shape=jax.ShapeDtypeStruct((ATOMS, CHANNELS), f32),
        in_specs=[pl.BlockSpec(memory_space=pltpu.VMEM)] * len(operands),
        out_specs=pl.BlockSpec(memory_space=pltpu.VMEM),
        scratch_shapes=[
            pltpu.VMEM((16, ATOMS), f32),
            pltpu.VMEM((16, WAVES), f32),
            pltpu.VMEM((WAVES, ATOMS), f32),
            pltpu.VMEM((ROWS, ATOMS), bf16),
            pltpu.VMEM((ROWS, ATOMS), bf16),
            pltpu.VMEM((CHANNELS, ATOMS), f32),
            pltpu.VMEM((2 * CHANNELS, ATOMS), bf16),
            pltpu.VMEM((BLOCKS, 2 * CHANNELS, CHANNELS), bf16),
            pltpu.VMEM((BLOCKS, 2 * CHANNELS, CHANNELS), bf16),
            pltpu.VMEM((BLOCKS, 2 * CHANNELS, CHANNELS), bf16),
            pltpu.VMEM((BLOCKS, CHANNELS, CHANNELS), f32),
            pltpu.VMEM((BLOCKS, CHUNKS, CHUNK, CHANNELS), f32),
            pltpu.VMEM((BLOCKS, CHUNKS, CHUNK, CHANNELS), f32),
            pltpu.VMEM((BLOCKS, CHUNKS, CHUNK, CHANNELS), f32),
            pltpu.VMEM((BLOCKS, CHUNKS, PLANE, PIECE, CHANNELS), f32),
            pltpu.VMEM((BLOCKS, CHUNKS, PIECE, CHANNELS), f32),
            pltpu.VMEM((BLOCKS, CHUNKS, NZ, PIECE, CHANNELS), f32),
            pltpu.VMEM((BLOCKS, ROWS, CHANNELS), f32),
            pltpu.VMEM((CHANNELS, ATOMS), f32),
            *sems,
        ],
        compiler_params=pltpu.CompilerParams(
            collective_id=0 if comm else None,
            has_side_effects=True,
            vmem_limit_bytes=56 << 20,
        ),
    )(*operands)


def solution(mesh):
    rows = P(("outer", "atoms"), None)
    return jax.shard_map(
        local,
        mesh=mesh,
        in_specs=(rows, P(None, ("outer", "atoms")), *[P()] * 7),
        out_specs=rows,
        check_vma=False,
    )
```

```python
import functools

import jax
import jax.numpy as jnp
from jax import lax
from jax.experimental import pallas as pl
from jax.experimental.pallas import tpu as pltpu
from jax.sharding import PartitionSpec as P

MESH = pl.DeviceIdType.MESH
f32 = jnp.float32
bf16 = jnp.bfloat16

NX, NY, NZ = 4, 4, 8
PLANE = NX * NY
ATOMS, CHANNELS, WAVES, BLOCKS = 1024, 128, 768, 2
ROWS = 2 * WAVES
HALF = ROWS // 2
CHUNKS = 3
CHUNK = HALF // CHUNKS
PIECE = CHUNK // PLANE
TURN = 262144.0
GROUP = 32
TAIL = ((0, CHUNKS - 1), (CHUNKS - 1, CHUNKS))

SIN = (4.442882834149947, -7.308241154547219, 3.6062889582380353, -0.8457635962127477, 0.10920575375428615)
COS = (1.4142134965650266, -6.978850988240709, 5.739461170716688, -1.8835629875263915, 0.31069819226115863)


def horner(coefficients, u):
    total = jnp.full_like(u, coefficients[-1])
    for c in coefficients[-2::-1]:
        total = total * u + c
    return total


def split(value):
    high = value.astype(bf16)
    return high, (value - high.astype(f32)).astype(bf16)


def dot(a, b):
    return jnp.dot(a, b, preferred_element_type=f32)


def dot_nt(a, b):
    return lax.dot_general(a, b, (((1,), (1,)), ((), ())), preferred_element_type=f32)


def hops(delta, size):
    return min(delta, size - delta)


PLANE_PEERS = sorted(
    ((dx, dy) for dx in range(NX) for dy in range(NY) if dx or dy),
    key=lambda d: -(hops(d[0], NX) + hops(d[1], NY)),
)
Z_PEERS = sorted(range(1, NZ), key=lambda d: -hops(d, NZ))


def body(
    feat_hbm, pos_hbm, wave_hbm, wv_hbm, filt_hbm, gain_hbm, wh_hbm, bh_hbm, wo_hbm,
    out_ref,
    feat_ref, pos_ref, wave_ref, wv_ref, filt_ref, gain_ref, wh_ref, bh_ref, wo_ref,
    xs_ref, ws_ref, turn_ref, high_ref, low_ref, cur_ref, proj_ref, wvt_ref, wht_ref, wot_ref, bht_ref,
    away_ref, home_ref, cross_ref, plane_ref, mine_ref, depth_ref, fact_ref, acc_ref,
    load_sem,
    cross_send, cross_recv, plane_send, plane_recv, depth_send, depth_recv,
    spread_send, spread_recv, pair_send, pair_recv,
    *, comm,
):
    loads = [
        pltpu.make_async_copy(source, target, load_sem.at[i])
        for i, (source, target) in enumerate(
            (
                (pos_hbm, pos_ref), (wave_hbm, wave_ref), (feat_hbm, feat_ref), (wv_hbm, wv_ref), (gain_hbm, gain_ref),
                (wh_hbm, wh_ref), (bh_hbm, bh_ref), (wo_hbm, wo_ref), (filt_hbm, filt_ref),
            )
        )
    ]
    for copy in loads:
        copy.start()

    outer, atoms = lax.axis_index("outer"), lax.axis_index("atoms")
    core, y = outer % 2, (atoms % 2) * 2 + outer // 2
    x, z = (atoms // 2) % NX, atoms // (2 * NX)
    me = x * NY + y

    def device(x, y, z, core):
        return ((y % 2) * 2 + core, z * (2 * NX) + x * 2 + y // 2)

    def plane_peer(delta):
        px, py = (x + delta[0]) % NX, (y + delta[1]) % NY
        return px * NY + py, device(px, py, z, core)

    other_core = device(x, y, z, 1 - core)

    def z_peer(delta):
        return device(x, y, (z + delta) % NZ, core)

    def send(source, target, send_sem, recv_sem, to):
        if comm:
            pltpu.make_async_remote_copy(
                src_ref=source, dst_ref=target, send_sem=send_sem, recv_sem=recv_sem,
                device_id=to, device_id_type=MESH,
            ).start()

    def wait(like, sem):
        if comm:
            pltpu.make_async_copy(like, like, sem).wait()

    if comm:
        barrier = pltpu.get_barrier_semaphore()
        for delta in PLANE_PEERS:
            pl.semaphore_signal(barrier, 1, device_id=plane_peer(delta)[1], device_id_type=MESH)
        for delta in Z_PEERS:
            pl.semaphore_signal(barrier, 1, device_id=z_peer(delta), device_id_type=MESH)
        pl.semaphore_signal(barrier, 1, device_id=other_core, device_id_type=MESH)

    for copy in loads[:2]:
        copy.wait()
    positions = pos_ref[...]
    waves = wave_ref[...].astype(f32)
    xs_ref[...] = jnp.zeros_like(xs_ref)
    ws_ref[...] = jnp.zeros_like(ws_ref)
    for i in range(3):
        xs_ref[3 * i : 3 * i + 3, :] = ((positions >> (8 * i)) & 255).astype(f32)
        ws_ref[3 * i : 3 * i + 3, :] = waves * (256.0**i / TURN)
    turn_ref[...] = dot(ws_ref[...].T.astype(bf16), xs_ref[...].astype(bf16))

    def transposed(matrix, held, b):
        high, low = split(matrix.T)
        held[b, :CHANNELS, :] = high
        held[b, CHANNELS:, :] = low

    def weighted(held, b, value):
        high, low = split(value)
        both = dot(held[b], high)
        return both[:CHANNELS] + both[CHANNELS:] + dot(held[b, :CHANNELS, :], low)

    def project(b):
        high, low = split(weighted(wvt_ref, b, cur_ref[...]).T)
        proj_ref[:, :CHANNELS] = high
        proj_ref[:, CHANNELS:] = low

    def chunk_rows(chunk):
        return pl.ds(pl.multiple_of(chunk * CHUNK, CHUNK), CHUNK)

    def table(chunk):
        def step(i, _):
            for j in range(GROUP // 16):
                octet = chunk * (CHUNK // 16) + i * (GROUP // 16) + j
                t = turn_ref[pl.ds(pl.multiple_of(octet * 8, 8), 8), :]
                r = t - jnp.round(t)
                u = r * r
                s = horner(SIN, u) * r
                high, low = split(jnp.concatenate([1.0 - s * s, s * horner(COS, u)], axis=0))
                at = pl.ds(pl.multiple_of(octet * 16, 16), 16)
                high_ref[at, :] = high
                low_ref[at, :] = low
            return 0

        lax.fori_loop(0, CHUNK // GROUP, step, 0)

    def factor(rows):
        a = dot(high_ref[rows, :], proj_ref[...])
        b = dot(low_ref[rows, :], proj_ref[...])
        return (a[:, :CHANNELS] + a[:, CHANNELS:]) + (b[:, :CHANNELS] + b[:, CHANNELS:])

    for copy in loads[2:4]:
        copy.wait()
    for b in range(BLOCKS):
        transposed(wv_ref[b], wvt_ref, b)
    cur_ref[...] = feat_ref[...].T
    project(0)
    for b in range(BLOCKS):
        order = [(1 - core) * CHUNKS + q for q in range(CHUNKS)] + [core * CHUNKS + q for q in range(CHUNKS)]
        if b == 0:
            table(order[0])
        for k, chunk in enumerate(order):
            q = k % CHUNKS
            part_ref = away_ref.at[b, q] if k < CHUNKS else home_ref.at[b, q]
            part_ref[...] = factor(chunk_rows(chunk))
            if b == 0 and k + 1 < len(order):
                table(order[k + 1])
            if k < CHUNKS:
                if comm and b == 0 and q == 0:
                    pl.semaphore_wait(barrier, len(PLANE_PEERS) + len(Z_PEERS) + 1)
                send(part_ref, cross_ref.at[b, q], cross_send.at[b, q], cross_recv.at[b, q], other_core)
            else:
                wait(cross_ref.at[b, q], cross_recv.at[b, q])
                part_ref[...] += cross_ref[b, q]
                for delta in PLANE_PEERS:
                    peer, to = plane_peer(delta)
                    send(
                        home_ref.at[b, q, pl.ds(pl.multiple_of(peer * PIECE, 8), PIECE)],
                        plane_ref.at[b, q, me], plane_send.at[b, q], plane_recv.at[b, q], to,
                    )
                plane_ref[b, q, me] = home_ref[b, q, pl.ds(pl.multiple_of(me * PIECE, 8), PIECE)]
        if b == 0:
            for copy in loads[4:]:
                copy.wait()
            for i in range(BLOCKS):
                transposed(wh_ref[i] * gain_ref[i : i + 1, :].T, wht_ref, i)
                transposed(wo_ref[i], wot_ref, i)
                bht_ref[i] = jnp.broadcast_to(bh_ref[i : i + 1, :], (CHANNELS, CHANNELS)).T
        for q in range(CHUNKS):
            wait(plane_ref.at[b, q, pl.ds(0, PLANE - 1)], plane_recv.at[b, q])
            mine_ref[b, q] = jnp.sum(plane_ref[b, q], axis=0)
            for delta in Z_PEERS:
                send(mine_ref.at[b, q], depth_ref.at[b, q, z], depth_send.at[b, q], depth_recv.at[b, q], z_peer(delta))
            depth_ref[b, q, z] = mine_ref[b, q]
        for q in range(CHUNKS):
            wait(depth_ref.at[b, q, pl.ds(0, NZ - 1)], depth_recv.at[b, q])
            total = jnp.sum(depth_ref[b, q], axis=0)
            first = (core * CHUNKS + q) * CHUNK + me * PIECE
            parts = []
            for i in range(PIECE // 8):
                octet = (first // 8 + i) // 2
                parts.append(filt_ref[b, pl.ds(pl.multiple_of(octet * 8, 8), 8), :])
            here = fact_ref.at[b, pl.ds(pl.multiple_of(first, 8), PIECE)]
            here[...] = total * jnp.concatenate(parts, axis=0)
            for delta in PLANE_PEERS:
                send(here, here, spread_send.at[b, q], spread_recv.at[b, q], plane_peer(delta)[1])
        for q in range(CHUNKS):
            chunk = pl.ds(pl.multiple_of((core * CHUNKS + q) * CHUNK, CHUNK), CHUNK)
            wait(fact_ref.at[b, pl.ds(0, (PLANE - 1) * PIECE)], spread_recv.at[b, q])
            whole = fact_ref.at[b, chunk]
            send(whole, whole, pair_send.at[b, q], pair_recv.at[b, q], other_core)
        def message(rows):
            high, low = split(fact_ref[b, rows, :].T)
            both = dot(jnp.concatenate([high, low], axis=0), high_ref[rows, :])
            return both[:CHANNELS] + both[CHANNELS:] + dot(high, low_ref[rows, :])

        acc_ref[...] = message(pl.ds(pl.multiple_of(core * HALF, HALF), HALF))
        for first, last in TAIL:
            for q in range(first, last):
                wait(fact_ref.at[b, pl.ds(0, CHUNK)], pair_recv.at[b, q])
            acc_ref[...] += message(pl.ds(pl.multiple_of((1 - core) * HALF + first * CHUNK, 128), (last - first) * CHUNK))
        messages = acc_ref[...]
        scale = lax.rsqrt(jnp.mean(messages * messages, axis=0, keepdims=True) + 1e-6)
        bias = jnp.concatenate([bht_ref[b]] * (ATOMS // CHANNELS), axis=1)
        v = weighted(wht_ref, b, messages) * scale + bias
        hidden = v / (1.0 + jnp.exp(-v))
        cur_ref[...] += weighted(wot_ref, b, hidden)
        if b + 1 < BLOCKS:
            project(b + 1)
    out_ref[...] = cur_ref[...].T
    for b in range(BLOCKS):
        for q in range(CHUNKS):
            wait(away_ref.at[b, q], cross_send.at[b, q])
            wait(plane_ref.at[b, q, pl.ds(0, PLANE - 1)], plane_send.at[b, q])
            wait(depth_ref.at[b, q, pl.ds(0, NZ - 1)], depth_send.at[b, q])
            wait(fact_ref.at[b, pl.ds(0, (PLANE - 1) * PIECE)], spread_send.at[b, q])
            wait(fact_ref.at[b, pl.ds(0, CHUNK)], pair_send.at[b, q])


def local(*operands, comm=True):
    sems = [pltpu.SemaphoreType.DMA((BLOCKS, CHUNKS))] * 10
    return pl.pallas_call(
        functools.partial(body, comm=comm),
        name="ewald",
        out_shape=pltpu.VMEM((ATOMS, CHANNELS), f32),
        in_specs=[pl.BlockSpec(memory_space=pltpu.HBM)] * len(operands),
        out_specs=pl.BlockSpec(memory_space=pltpu.VMEM),
        scratch_shapes=[
            *[pltpu.VMEM(operand.shape, operand.dtype) for operand in operands],
            pltpu.VMEM((16, ATOMS), f32),
            pltpu.VMEM((16, WAVES), f32),
            pltpu.VMEM((WAVES, ATOMS), f32),
            pltpu.VMEM((ROWS, ATOMS), bf16),
            pltpu.VMEM((ROWS, ATOMS), bf16),
            pltpu.VMEM((CHANNELS, ATOMS), f32),
            pltpu.VMEM((ATOMS, 2 * CHANNELS), bf16),
            pltpu.VMEM((BLOCKS, 2 * CHANNELS, CHANNELS), bf16),
            pltpu.VMEM((BLOCKS, 2 * CHANNELS, CHANNELS), bf16),
            pltpu.VMEM((BLOCKS, 2 * CHANNELS, CHANNELS), bf16),
            pltpu.VMEM((BLOCKS, CHANNELS, CHANNELS), f32),
            pltpu.VMEM((BLOCKS, CHUNKS, CHUNK, CHANNELS), f32),
            pltpu.VMEM((BLOCKS, CHUNKS, CHUNK, CHANNELS), f32),
            pltpu.VMEM((BLOCKS, CHUNKS, CHUNK, CHANNELS), f32),
            pltpu.VMEM((BLOCKS, CHUNKS, PLANE, PIECE, CHANNELS), f32),
            pltpu.VMEM((BLOCKS, CHUNKS, PIECE, CHANNELS), f32),
            pltpu.VMEM((BLOCKS, CHUNKS, NZ, PIECE, CHANNELS), f32),
            pltpu.VMEM((BLOCKS, ROWS, CHANNELS), f32),
            pltpu.VMEM((CHANNELS, ATOMS), f32),
            pltpu.SemaphoreType.DMA((9,)),
            *sems,
        ],
        compiler_params=pltpu.CompilerParams(
            collective_id=0 if comm else None,
            has_side_effects=True,
            vmem_limit_bytes=56 << 20,
        ),
    )(*operands)


def solution(mesh):
    rows = P(("outer", "atoms"), None)
    return jax.shard_map(
        local,
        mesh=mesh,
        in_specs=(rows, P(None, ("outer", "atoms")), *[P()] * 7),
        out_specs=rows,
        check_vma=False,
    )
```

```python
import functools

import jax
import jax.numpy as jnp
from jax import lax
from jax.experimental import pallas as pl
from jax.experimental.pallas import tpu as pltpu
from jax.sharding import PartitionSpec as P

MESH = pl.DeviceIdType.MESH
f32 = jnp.float32
bf16 = jnp.bfloat16

NX, NY, NZ = 4, 4, 8
PLANE = NX * NY
ATOMS, CHANNELS, WAVES, BLOCKS = 1024, 128, 768, 2
ROWS = 2 * WAVES
HALF = ROWS // 2
CHUNKS = 3
CHUNK = HALF // CHUNKS
PIECE = CHUNK // PLANE
TURN = 262144.0
FUSED = 256
GROUP = 32
TAIL = ((0, CHUNKS - 1), (CHUNKS - 1, CHUNKS))

SIN = (4.442882834149947, -7.308241154547219, 3.6062889582380353, -0.8457635962127477, 0.10920575375428615)
COS = (1.4142134965650266, -6.978850988240709, 5.739461170716688, -1.8835629875263915, 0.31069819226115863)


def horner(coefficients, u):
    total = jnp.full_like(u, coefficients[-1])
    for c in coefficients[-2::-1]:
        total = total * u + c
    return total


def split(value):
    high = value.astype(bf16)
    return high, (value - high.astype(f32)).astype(bf16)


def dot(a, b):
    return jnp.dot(a, b, preferred_element_type=f32)


def dot_nt(a, b):
    return lax.dot_general(a, b, (((1,), (1,)), ((), ())), preferred_element_type=f32)


def hops(delta, size):
    return min(delta, size - delta)


PLANE_PEERS = sorted(
    ((dx, dy) for dx in range(NX) for dy in range(NY) if dx or dy),
    key=lambda d: -(hops(d[0], NX) + hops(d[1], NY)),
)
Z_PEERS = sorted(range(1, NZ), key=lambda d: -hops(d, NZ))


def body(
    feat_hbm, pos_hbm, wave_hbm, wv_hbm, filt_hbm, gain_hbm, wh_hbm, bh_hbm, wo_hbm,
    out_ref,
    feat_ref, pos_ref, wave_ref, wv_ref, filt_ref, gain_ref, wh_ref, bh_ref, wo_ref,
    xs_ref, ws_ref, turn_ref, high_ref, low_ref, cur_ref, proj_ref, wvt_ref, wht_ref, wot_ref, bht_ref,
    away_ref, home_ref, cross_ref, plane_ref, mine_ref, depth_ref, fact_ref, acc_ref,
    load_sem,
    cross_send, cross_recv, plane_send, plane_recv, depth_send, depth_recv,
    spread_send, spread_recv, pair_send, pair_recv,
    *, comm,
):
    loads = [
        pltpu.make_async_copy(source, target, load_sem.at[i])
        for i, (source, target) in enumerate(
            (
                (pos_hbm, pos_ref), (wave_hbm, wave_ref), (feat_hbm, feat_ref), (wv_hbm, wv_ref), (gain_hbm, gain_ref),
                (wh_hbm, wh_ref), (bh_hbm, bh_ref), (wo_hbm, wo_ref), (filt_hbm, filt_ref),
            )
        )
    ]
    for copy in loads:
        copy.start()

    outer, atoms = lax.axis_index("outer"), lax.axis_index("atoms")
    core, y = outer % 2, (atoms % 2) * 2 + outer // 2
    x, z = (atoms // 2) % NX, atoms // (2 * NX)
    me = x * NY + y

    def device(x, y, z, core):
        return ((y % 2) * 2 + core, z * (2 * NX) + x * 2 + y // 2)

    def plane_peer(delta):
        px, py = (x + delta[0]) % NX, (y + delta[1]) % NY
        return px * NY + py, device(px, py, z, core)

    other_core = device(x, y, z, 1 - core)

    def z_peer(delta):
        return device(x, y, (z + delta) % NZ, core)

    def send(source, target, send_sem, recv_sem, to):
        if comm:
            pltpu.make_async_remote_copy(
                src_ref=source, dst_ref=target, send_sem=send_sem, recv_sem=recv_sem,
                device_id=to, device_id_type=MESH,
            ).start()

    def wait(like, sem):
        if comm:
            pltpu.make_async_copy(like, like, sem).wait()

    if comm:
        barrier = pltpu.get_barrier_semaphore()
        for delta in PLANE_PEERS:
            pl.semaphore_signal(barrier, 1, device_id=plane_peer(delta)[1], device_id_type=MESH)
        for delta in Z_PEERS:
            pl.semaphore_signal(barrier, 1, device_id=z_peer(delta), device_id_type=MESH)
        pl.semaphore_signal(barrier, 1, device_id=other_core, device_id_type=MESH)

    for copy in loads[:2]:
        copy.wait()
    positions = pos_ref[...]
    waves = wave_ref[...].astype(f32)
    xs_ref[...] = jnp.zeros_like(xs_ref)
    ws_ref[...] = jnp.zeros_like(ws_ref)
    for i in range(3):
        xs_ref[3 * i : 3 * i + 3, :] = ((positions >> (8 * i)) & 255).astype(f32)
        ws_ref[3 * i : 3 * i + 3, :] = waves * (256.0**i / TURN)
    turn_ref[...] = dot(ws_ref[...].T.astype(bf16), xs_ref[...].astype(bf16))

    def transposed(matrix, held, b):
        high, low = split(matrix.T)
        held[b, :CHANNELS, :] = high
        held[b, CHANNELS:, :] = low

    def weighted(held, b, value):
        high, low = split(value)
        both = dot(held[b], high)
        return both[:CHANNELS] + both[CHANNELS:] + dot(held[b, :CHANNELS, :], low)

    def project(b):
        high, low = split(weighted(wvt_ref, b, cur_ref[...]).T)
        proj_ref[:, :CHANNELS] = high
        proj_ref[:, CHANNELS:] = low

    def chunk_rows(chunk):
        return pl.ds(pl.multiple_of(chunk * CHUNK, CHUNK), CHUNK)

    def table(chunk):
        table_rows(chunk, 0, CHUNK)

    def table_rows(chunk, i, group):
            for j in range(group // 16):
                octet = chunk * (CHUNK // 16) + i * (group // 16) + j
                t = turn_ref[pl.ds(pl.multiple_of(octet * 8, 8), 8), :]
                r = t - jnp.round(t)
                u = r * r
                s = horner(SIN, u) * r
                high, low = split(jnp.concatenate([1.0 - s * s, s * horner(COS, u)], axis=0))
                at = pl.ds(pl.multiple_of(octet * 16, 16), 16)
                high_ref[at, :] = high
                low_ref[at, :] = low

    def factor(rows):
        a = dot(high_ref[rows, :], proj_ref[...])
        b = dot(low_ref[rows, :], proj_ref[:, :CHANNELS])
        return (a[:, :CHANNELS] + a[:, CHANNELS:]) + b

    def hand_over(b, q):
        send(away_ref.at[b, q], cross_ref.at[b, q], cross_send.at[b, q], cross_recv.at[b, q], other_core)

    def reduce_plane(b, q):
        wait(cross_ref.at[b, q], cross_recv.at[b, q])
        home_ref[b, q] += cross_ref[b, q]
        for delta in PLANE_PEERS:
            peer, to = plane_peer(delta)
            send(
                home_ref.at[b, q, pl.ds(pl.multiple_of(peer * PIECE, 8), PIECE)],
                plane_ref.at[b, q, me], plane_send.at[b, q], plane_recv.at[b, q], to,
            )
        plane_ref[b, q, me] = home_ref[b, q, pl.ds(pl.multiple_of(me * PIECE, 8), PIECE)]

    table((1 - core) * CHUNKS)
    for copy in loads[2:4]:
        copy.wait()
    high, low = split(feat_ref[...])
    weights = jnp.concatenate(split(wv_ref[0]), axis=1)
    both = dot(high, weights)
    high, low = split(both[:, :CHANNELS] + both[:, CHANNELS:] + dot(low, weights[:, :CHANNELS]))
    proj_ref[:, :CHANNELS] = high
    proj_ref[:, CHANNELS:] = low
    for b in range(BLOCKS):
        order = [(1 - core) * CHUNKS + q for q in range(CHUNKS)] + [core * CHUNKS + q for q in range(CHUNKS)]
        for k, chunk in enumerate(order):
            q = k % CHUNKS
            part_ref = away_ref.at[b, q] if k < CHUNKS else home_ref.at[b, q]
            if b == 0 and k + 1 < len(order):

                def step(i, _, chunk=chunk, part_ref=part_ref, following=order[k + 1]):
                    rows = pl.ds(pl.multiple_of(chunk * CHUNK + i * FUSED, FUSED), FUSED)
                    part = factor(rows)
                    table_rows(following, i, FUSED)
                    part_ref[pl.ds(pl.multiple_of(i * FUSED, FUSED), FUSED), :] = part
                    return 0

                lax.fori_loop(0, CHUNK // FUSED, step, 0)
            else:
                part_ref[...] = factor(chunk_rows(chunk))
            if b:
                ready = [k]
            elif k < CHUNKS - 1:
                ready = []
            elif k == CHUNKS - 1:
                if comm:
                    pl.semaphore_wait(barrier, len(PLANE_PEERS) + len(Z_PEERS) + 1)
                ready = list(range(CHUNKS))
            else:
                ready = [k]
            for j in ready:
                if j < CHUNKS:
                    hand_over(b, j)
                else:
                    reduce_plane(b, j - CHUNKS)
        if b == 0:
            for copy in loads[4:]:
                copy.wait()
            cur_ref[...] = feat_ref[...].T
            for i in range(BLOCKS):
                if i:
                    transposed(wv_ref[i], wvt_ref, i)
                transposed(wh_ref[i] * gain_ref[i : i + 1, :].T, wht_ref, i)
                transposed(wo_ref[i], wot_ref, i)
                bht_ref[i] = jnp.broadcast_to(bh_ref[i : i + 1, :], (CHANNELS, CHANNELS)).T
        for q in range(CHUNKS):
            wait(plane_ref.at[b, q, pl.ds(0, PLANE - 1)], plane_recv.at[b, q])
            mine_ref[b, q] = jnp.sum(plane_ref[b, q], axis=0)
            for delta in Z_PEERS:
                send(mine_ref.at[b, q], depth_ref.at[b, q, z], depth_send.at[b, q], depth_recv.at[b, q], z_peer(delta))
            depth_ref[b, q, z] = mine_ref[b, q]
        for q in range(CHUNKS):
            wait(depth_ref.at[b, q, pl.ds(0, NZ - 1)], depth_recv.at[b, q])
            total = jnp.sum(depth_ref[b, q], axis=0)
            first = (core * CHUNKS + q) * CHUNK + me * PIECE
            parts = []
            for i in range(PIECE // 8):
                octet = (first // 8 + i) // 2
                parts.append(filt_ref[b, pl.ds(pl.multiple_of(octet * 8, 8), 8), :])
            here = fact_ref.at[b, pl.ds(pl.multiple_of(first, 8), PIECE)]
            here[...] = total * jnp.concatenate(parts, axis=0)
            for delta in PLANE_PEERS:
                send(here, here, spread_send.at[b, q], spread_recv.at[b, q], plane_peer(delta)[1])
        for q in range(CHUNKS):
            chunk = pl.ds(pl.multiple_of((core * CHUNKS + q) * CHUNK, CHUNK), CHUNK)
            wait(fact_ref.at[b, pl.ds(0, (PLANE - 1) * PIECE)], spread_recv.at[b, q])
            whole = fact_ref.at[b, chunk]
            send(whole, whole, pair_send.at[b, q], pair_recv.at[b, q], other_core)
        def message(rows):
            high, low = split(fact_ref[b, rows, :].T)
            both = dot(jnp.concatenate([high, low], axis=0), high_ref[rows, :])
            return both[:CHANNELS] + both[CHANNELS:] + dot(high, low_ref[rows, :])

        acc_ref[...] = message(pl.ds(pl.multiple_of(core * HALF, HALF), HALF))
        for first, last in TAIL:
            for q in range(first, last):
                wait(fact_ref.at[b, pl.ds(0, CHUNK)], pair_recv.at[b, q])
            acc_ref[...] += message(pl.ds(pl.multiple_of((1 - core) * HALF + first * CHUNK, 128), (last - first) * CHUNK))
        messages = acc_ref[...]
        scale = lax.rsqrt(jnp.mean(messages * messages, axis=0, keepdims=True) + 1e-6)
        bias = jnp.concatenate([bht_ref[b]] * (ATOMS // CHANNELS), axis=1)
        v = weighted(wht_ref, b, messages) * scale + bias
        hidden = v / (1.0 + jnp.exp(-v))
        cur_ref[...] += weighted(wot_ref, b, hidden)
        if b + 1 < BLOCKS:
            project(b + 1)
    out_ref[...] = cur_ref[...].T
    for b in range(BLOCKS):
        for q in range(CHUNKS):
            wait(away_ref.at[b, q], cross_send.at[b, q])
            wait(plane_ref.at[b, q, pl.ds(0, PLANE - 1)], plane_send.at[b, q])
            wait(depth_ref.at[b, q, pl.ds(0, NZ - 1)], depth_send.at[b, q])
            wait(fact_ref.at[b, pl.ds(0, (PLANE - 1) * PIECE)], spread_send.at[b, q])
            wait(fact_ref.at[b, pl.ds(0, CHUNK)], pair_send.at[b, q])


def local(*operands, comm=True):
    sems = [pltpu.SemaphoreType.DMA((BLOCKS, CHUNKS))] * 10
    return pl.pallas_call(
        functools.partial(body, comm=comm),
        name="ewald",
        out_shape=pltpu.VMEM((ATOMS, CHANNELS), f32),
        in_specs=[pl.BlockSpec(memory_space=pltpu.HBM)] * len(operands),
        out_specs=pl.BlockSpec(memory_space=pltpu.VMEM),
        scratch_shapes=[
            *[pltpu.VMEM(operand.shape, operand.dtype) for operand in operands],
            pltpu.VMEM((16, ATOMS), f32),
            pltpu.VMEM((16, WAVES), f32),
            pltpu.VMEM((WAVES, ATOMS), f32),
            pltpu.VMEM((ROWS, ATOMS), bf16),
            pltpu.VMEM((ROWS, ATOMS), bf16),
            pltpu.VMEM((CHANNELS, ATOMS), f32),
            pltpu.VMEM((ATOMS, 2 * CHANNELS), bf16),
            pltpu.VMEM((BLOCKS, 2 * CHANNELS, CHANNELS), bf16),
            pltpu.VMEM((BLOCKS, 2 * CHANNELS, CHANNELS), bf16),
            pltpu.VMEM((BLOCKS, 2 * CHANNELS, CHANNELS), bf16),
            pltpu.VMEM((BLOCKS, CHANNELS, CHANNELS), f32),
            pltpu.VMEM((BLOCKS, CHUNKS, CHUNK, CHANNELS), f32),
            pltpu.VMEM((BLOCKS, CHUNKS, CHUNK, CHANNELS), f32),
            pltpu.VMEM((BLOCKS, CHUNKS, CHUNK, CHANNELS), f32),
            pltpu.VMEM((BLOCKS, CHUNKS, PLANE, PIECE, CHANNELS), f32),
            pltpu.VMEM((BLOCKS, CHUNKS, PIECE, CHANNELS), f32),
            pltpu.VMEM((BLOCKS, CHUNKS, NZ, PIECE, CHANNELS), f32),
            pltpu.VMEM((BLOCKS, ROWS, CHANNELS), f32),
            pltpu.VMEM((CHANNELS, ATOMS), f32),
            pltpu.SemaphoreType.DMA((9,)),
            *sems,
        ],
        compiler_params=pltpu.CompilerParams(
            collective_id=0 if comm else None,
            has_side_effects=True,
            vmem_limit_bytes=56 << 20,
        ),
    )(*operands)


def solution(mesh):
    rows = P(("outer", "atoms"), None)
    return jax.shard_map(
        local,
        mesh=mesh,
        in_specs=(rows, P(None, ("outer", "atoms")), *[P()] * 7),
        out_specs=rows,
        check_vma=False,
    )
```

```python
import functools

import jax
import jax.numpy as jnp
from jax import lax
from jax.experimental import pallas as pl
from jax.experimental.pallas import tpu as pltpu
from jax.sharding import PartitionSpec as P

MESH = pl.DeviceIdType.MESH
f32 = jnp.float32
bf16 = jnp.bfloat16

NX, NY, NZ = 4, 4, 8
PLANE = NX * NY
ATOMS, CHANNELS, WAVES, BLOCKS = 1024, 128, 768, 2
ROWS = 2 * WAVES
HALF = ROWS // 2
CHUNKS = 3
CHUNK = HALF // CHUNKS
PIECE = CHUNK // PLANE
TURN = 262144.0
FUSED = 256
TAIL = ((0, CHUNKS - 1), (CHUNKS - 1, CHUNKS))

SIN = (4.442882834149947, -7.308241154547219, 3.6062889582380353, -0.8457635962127477, 0.10920575375428615)
COS = (1.4142134965650266, -6.978850988240709, 5.739461170716688, -1.8835629875263915, 0.31069819226115863)


def horner(coefficients, u):
    total = jnp.full_like(u, coefficients[-1])
    for c in coefficients[-2::-1]:
        total = total * u + c
    return total


def split(value):
    high = value.astype(bf16)
    return high, (value - high.astype(f32)).astype(bf16)


def dot(a, b):
    return jnp.dot(a, b, preferred_element_type=f32)


def dot_nt(a, b):
    return lax.dot_general(a, b, (((1,), (1,)), ((), ())), preferred_element_type=f32)


def hops(delta, size):
    return min(delta, size - delta)


PLANE_PEERS = sorted(
    ((dx, dy) for dx in range(NX) for dy in range(NY) if dx or dy),
    key=lambda d: -(hops(d[0], NX) + hops(d[1], NY)),
)
Z_PEERS = sorted(range(1, NZ), key=lambda d: -hops(d, NZ))


def body(
    feat_hbm, pos_hbm, wave_hbm, wv_hbm, filt_hbm, gain_hbm, wh_hbm, bh_hbm, wo_hbm,
    out_ref,
    feat_ref, pos_ref, wave_ref, wv_ref, filt_ref, gain_ref, wh_ref, bh_ref, wo_ref,
    xs_ref, ws_ref, turn_ref, high_ref, low_ref, cur_ref, proj_ref, wvt_ref, wht_ref, wot_ref, bht_ref,
    away_ref, home_ref, cross_ref, plane_ref, mine_ref, depth_ref, fact_ref, acc_ref,
    load_sem,
    cross_send, cross_recv, plane_send, plane_recv, depth_send, depth_recv,
    spread_send, spread_recv, pair_send, pair_recv,
    *, comm,
):
    loads = [
        pltpu.make_async_copy(source, target, load_sem.at[i])
        for i, (source, target) in enumerate(
            (
                (pos_hbm, pos_ref), (wave_hbm, wave_ref), (feat_hbm, feat_ref), (wv_hbm, wv_ref), (gain_hbm, gain_ref),
                (wh_hbm, wh_ref), (bh_hbm, bh_ref), (wo_hbm, wo_ref), (filt_hbm, filt_ref),
            )
        )
    ]
    for copy in loads:
        copy.start()

    outer, atoms = lax.axis_index("outer"), lax.axis_index("atoms")
    core, y = lax.rem(outer, 2), lax.rem(atoms, 2) * 2 + lax.div(outer, 2)
    x, z = lax.rem(lax.div(atoms, 2), NX), lax.div(atoms, 2 * NX)
    me = x * NY + y

    def device(x, y, z, core):
        return (lax.rem(y, 2) * 2 + core, z * (2 * NX) + x * 2 + lax.div(y, 2))

    plane_peers, z_peers = {}, {}
    for delta in PLANE_PEERS:
        px, py = lax.rem(x + delta[0], NX), lax.rem(y + delta[1], NY)
        plane_peers[delta] = (px * NY + py, device(px, py, z, core))
    for delta in Z_PEERS:
        z_peers[delta] = device(x, y, lax.rem(z + delta, NZ), core)

    def plane_peer(delta):
        return plane_peers[delta]

    other_core = device(x, y, z, 1 - core)

    def z_peer(delta):
        return z_peers[delta]

    def send(source, target, send_sem, recv_sem, to):
        if comm:
            pltpu.make_async_remote_copy(
                src_ref=source, dst_ref=target, send_sem=send_sem, recv_sem=recv_sem,
                device_id=to, device_id_type=MESH,
            ).start()

    def wait(like, sem):
        if comm:
            pltpu.make_async_copy(like, like, sem).wait()

    if comm:
        barrier = pltpu.get_barrier_semaphore()
        for delta in PLANE_PEERS:
            pl.semaphore_signal(barrier, 1, device_id=plane_peer(delta)[1], device_id_type=MESH)
        for delta in Z_PEERS:
            pl.semaphore_signal(barrier, 1, device_id=z_peer(delta), device_id_type=MESH)
        pl.semaphore_signal(barrier, 1, device_id=other_core, device_id_type=MESH)

    for copy in loads[:2]:
        copy.wait()
    positions = pos_ref[...]
    waves = wave_ref[...].astype(f32)
    xs_ref[...] = jnp.zeros_like(xs_ref)
    ws_ref[...] = jnp.zeros_like(ws_ref)
    for i in range(3):
        xs_ref[3 * i : 3 * i + 3, :] = ((positions >> (8 * i)) & 255).astype(f32)
        ws_ref[3 * i : 3 * i + 3, :] = waves * (256.0**i / TURN)
    turn_ref[...] = dot(ws_ref[...].T.astype(bf16), xs_ref[...].astype(bf16))

    def transposed(matrix, held, b):
        high, low = split(matrix.T)
        held[b, :CHANNELS, :] = high
        held[b, CHANNELS:, :] = low

    def weighted(held, b, value):
        high, low = split(value)
        both = dot(held[b], high)
        return both[:CHANNELS] + both[CHANNELS:] + dot(held[b, :CHANNELS, :], low)

    def project(b):
        high, low = split(weighted(wvt_ref, b, cur_ref[...]).T)
        proj_ref[:, :CHANNELS] = high
        proj_ref[:, CHANNELS:] = low

    def chunk_rows(chunk):
        return pl.ds(pl.multiple_of(chunk * CHUNK, CHUNK), CHUNK)

    def table(chunk):
        table_rows(chunk, 0, CHUNK)

    def table_rows(chunk, i, group):
        for j in range(group // 16):
            octet = chunk * (CHUNK // 16) + i * (group // 16) + j
            t = turn_ref[pl.ds(pl.multiple_of(octet * 8, 8), 8), :]
            r = t - jnp.round(t)
            u = r * r
            s = horner(SIN, u) * r
            high, low = split(jnp.concatenate([1.0 - s * s, s * horner(COS, u)], axis=0))
            at = pl.ds(pl.multiple_of(octet * 16, 16), 16)
            high_ref[at, :] = high
            low_ref[at, :] = low

    def factor(rows):
        a = dot(high_ref[rows, :], proj_ref[...])
        b = dot(low_ref[rows, :], proj_ref[:, :CHANNELS])
        return (a[:, :CHANNELS] + a[:, CHANNELS:]) + b

    def hand_over(b, q):
        send(away_ref.at[b, q], cross_ref.at[b, q], cross_send.at[b, q], cross_recv.at[b, q], other_core)

    def reduce_plane(b, q):
        wait(cross_ref.at[b, q], cross_recv.at[b, q])
        home_ref[b, q] += cross_ref[b, q]
        for delta in PLANE_PEERS:
            peer, to = plane_peer(delta)
            send(
                home_ref.at[b, q, pl.ds(pl.multiple_of(peer * PIECE, 8), PIECE)],
                plane_ref.at[b, q, me], plane_send.at[b, q], plane_recv.at[b, q], to,
            )
        plane_ref[b, q, me] = home_ref[b, q, pl.ds(pl.multiple_of(me * PIECE, 8), PIECE)]

    table((1 - core) * CHUNKS)
    for copy in loads[2:4]:
        copy.wait()
    high, low = split(feat_ref[...])
    weights = jnp.concatenate(split(wv_ref[0]), axis=1)
    both = dot(high, weights)
    high, low = split(both[:, :CHANNELS] + both[:, CHANNELS:] + dot(low, weights[:, :CHANNELS]))
    proj_ref[:, :CHANNELS] = high
    proj_ref[:, CHANNELS:] = low
    for b in range(BLOCKS):
        order = [(1 - core) * CHUNKS + q for q in range(CHUNKS)] + [core * CHUNKS + q for q in range(CHUNKS)]
        for k, chunk in enumerate(order):
            q = k % CHUNKS
            part_ref = away_ref.at[b, q] if k < CHUNKS else home_ref.at[b, q]
            if b == 0 and k + 1 < len(order):

                def step(i, _, chunk=chunk, part_ref=part_ref, following=order[k + 1]):
                    rows = pl.ds(pl.multiple_of(chunk * CHUNK + i * FUSED, FUSED), FUSED)
                    part = factor(rows)
                    table_rows(following, i, FUSED)
                    part_ref[pl.ds(pl.multiple_of(i * FUSED, FUSED), FUSED), :] = part
                    return 0

                lax.fori_loop(0, CHUNK // FUSED, step, 0)
            else:
                part_ref[...] = factor(chunk_rows(chunk))
            if b:
                ready = [k]
            elif k < CHUNKS - 1:
                ready = []
            elif k == CHUNKS - 1:
                if comm:
                    pl.semaphore_wait(barrier, len(PLANE_PEERS) + len(Z_PEERS) + 1)
                ready = list(range(CHUNKS))
            else:
                ready = [k]
            for j in ready:
                if j < CHUNKS:
                    hand_over(b, j)
                else:
                    reduce_plane(b, j - CHUNKS)
        if b == 0:
            for copy in loads[4:]:
                copy.wait()
            cur_ref[...] = feat_ref[...].T
            for i in range(BLOCKS):
                if i:
                    transposed(wv_ref[i], wvt_ref, i)
                transposed(wh_ref[i] * gain_ref[i : i + 1, :].T, wht_ref, i)
                transposed(wo_ref[i], wot_ref, i)
                bht_ref[i] = jnp.broadcast_to(bh_ref[i : i + 1, :], (CHANNELS, CHANNELS)).T
        for q in range(CHUNKS):
            wait(plane_ref.at[b, q, pl.ds(0, PLANE - 1)], plane_recv.at[b, q])
            mine_ref[b, q] = jnp.sum(plane_ref[b, q], axis=0)
            for delta in Z_PEERS:
                send(mine_ref.at[b, q], depth_ref.at[b, q, z], depth_send.at[b, q], depth_recv.at[b, q], z_peer(delta))
            depth_ref[b, q, z] = mine_ref[b, q]
        for q in range(CHUNKS):
            wait(depth_ref.at[b, q, pl.ds(0, NZ - 1)], depth_recv.at[b, q])
            total = jnp.sum(depth_ref[b, q], axis=0)
            first = (core * CHUNKS + q) * CHUNK + me * PIECE
            parts = []
            for i in range(PIECE // 8):
                octet = (first // 8 + i) // 2
                parts.append(filt_ref[b, pl.ds(pl.multiple_of(octet * 8, 8), 8), :])
            here = fact_ref.at[b, pl.ds(pl.multiple_of(first, 8), PIECE)]
            here[...] = total * jnp.concatenate(parts, axis=0)
            for delta in PLANE_PEERS:
                send(here, here, spread_send.at[b, q], spread_recv.at[b, q], plane_peer(delta)[1])
        for q in range(CHUNKS):
            chunk = pl.ds(pl.multiple_of((core * CHUNKS + q) * CHUNK, CHUNK), CHUNK)
            wait(fact_ref.at[b, pl.ds(0, (PLANE - 1) * PIECE)], spread_recv.at[b, q])
            whole = fact_ref.at[b, chunk]
            send(whole, whole, pair_send.at[b, q], pair_recv.at[b, q], other_core)
        def message(rows):
            high, low = split(fact_ref[b, rows, :].T)
            both = dot(jnp.concatenate([high, low], axis=0), high_ref[rows, :])
            return both[:CHANNELS] + both[CHANNELS:] + dot(high, low_ref[rows, :])

        acc_ref[...] = message(pl.ds(pl.multiple_of(core * HALF, HALF), HALF))
        for first, last in TAIL:
            for q in range(first, last):
                wait(fact_ref.at[b, pl.ds(0, CHUNK)], pair_recv.at[b, q])
            acc_ref[...] += message(pl.ds(pl.multiple_of((1 - core) * HALF + first * CHUNK, 128), (last - first) * CHUNK))
        messages = acc_ref[...]
        scale = lax.rsqrt(jnp.mean(messages * messages, axis=0, keepdims=True) + 1e-6)
        bias = jnp.concatenate([bht_ref[b]] * (ATOMS // CHANNELS), axis=1)
        v = weighted(wht_ref, b, messages) * scale + bias
        hidden = v / (1.0 + jnp.exp(-v))
        cur_ref[...] += weighted(wot_ref, b, hidden)
        if b + 1 < BLOCKS:
            project(b + 1)
    out_ref[...] = cur_ref[...].T
    for b in range(BLOCKS):
        for q in range(CHUNKS):
            wait(away_ref.at[b, q], cross_send.at[b, q])
            wait(plane_ref.at[b, q, pl.ds(0, PLANE - 1)], plane_send.at[b, q])
            wait(depth_ref.at[b, q, pl.ds(0, NZ - 1)], depth_send.at[b, q])
            wait(fact_ref.at[b, pl.ds(0, (PLANE - 1) * PIECE)], spread_send.at[b, q])
            wait(fact_ref.at[b, pl.ds(0, CHUNK)], pair_send.at[b, q])


def local(*operands, comm=True):
    sems = [pltpu.SemaphoreType.DMA((BLOCKS, CHUNKS))] * 10
    return pl.pallas_call(
        functools.partial(body, comm=comm),
        name="ewald",
        out_shape=pltpu.VMEM((ATOMS, CHANNELS), f32),
        in_specs=[pl.BlockSpec(memory_space=pltpu.HBM)] * len(operands),
        out_specs=pl.BlockSpec(memory_space=pltpu.VMEM),
        scratch_shapes=[
            *[pltpu.VMEM(operand.shape, operand.dtype) for operand in operands],
            pltpu.VMEM((16, ATOMS), f32),
            pltpu.VMEM((16, WAVES), f32),
            pltpu.VMEM((WAVES, ATOMS), f32),
            pltpu.VMEM((ROWS, ATOMS), bf16),
            pltpu.VMEM((ROWS, ATOMS), bf16),
            pltpu.VMEM((CHANNELS, ATOMS), f32),
            pltpu.VMEM((ATOMS, 2 * CHANNELS), bf16),
            pltpu.VMEM((BLOCKS, 2 * CHANNELS, CHANNELS), bf16),
            pltpu.VMEM((BLOCKS, 2 * CHANNELS, CHANNELS), bf16),
            pltpu.VMEM((BLOCKS, 2 * CHANNELS, CHANNELS), bf16),
            pltpu.VMEM((BLOCKS, CHANNELS, CHANNELS), f32),
            pltpu.VMEM((BLOCKS, CHUNKS, CHUNK, CHANNELS), f32),
            pltpu.VMEM((BLOCKS, CHUNKS, CHUNK, CHANNELS), f32),
            pltpu.VMEM((BLOCKS, CHUNKS, CHUNK, CHANNELS), f32),
            pltpu.VMEM((BLOCKS, CHUNKS, PLANE, PIECE, CHANNELS), f32),
            pltpu.VMEM((BLOCKS, CHUNKS, PIECE, CHANNELS), f32),
            pltpu.VMEM((BLOCKS, CHUNKS, NZ, PIECE, CHANNELS), f32),
            pltpu.VMEM((BLOCKS, ROWS, CHANNELS), f32),
            pltpu.VMEM((CHANNELS, ATOMS), f32),
            pltpu.SemaphoreType.DMA((9,)),
            *sems,
        ],
        compiler_params=pltpu.CompilerParams(
            collective_id=0 if comm else None,
            has_side_effects=True,
            vmem_limit_bytes=56 << 20,
        ),
    )(*operands)


def solution(mesh):
    rows = P(("outer", "atoms"), None)
    return jax.shard_map(
        local,
        mesh=mesh,
        in_specs=(rows, P(None, ("outer", "atoms")), *[P()] * 7),
        out_specs=rows,
        check_vma=False,
    )
```

```python
import functools

import jax
import jax.numpy as jnp
from jax import lax
from jax.experimental import pallas as pl
from jax.experimental.pallas import tpu as pltpu
from jax.sharding import PartitionSpec as P

MESH = pl.DeviceIdType.MESH
f32 = jnp.float32
bf16 = jnp.bfloat16

NX, NY, NZ = 4, 4, 8
PLANE = NX * NY
ATOMS, CHANNELS, WAVES, BLOCKS = 1024, 128, 768, 2
ROWS = 2 * WAVES
HALF = ROWS // 2
CHUNKS = 3
CHUNK = HALF // CHUNKS
PIECE = CHUNK // PLANE
TURN = 262144.0
FUSED = 256
TAIL = ((0, CHUNKS - 1), (CHUNKS - 1, CHUNKS))

SIN = (4.442882834149947, -7.308241154547219, 3.6062889582380353, -0.8457635962127477, 0.10920575375428615)
COS = (1.4142134965650266, -6.978850988240709, 5.739461170716688, -1.8835629875263915, 0.31069819226115863)


def horner(coefficients, u):
    total = jnp.full_like(u, coefficients[-1])
    for c in coefficients[-2::-1]:
        total = total * u + c
    return total


def split(value):
    high = value.astype(bf16)
    return high, (value - high.astype(f32)).astype(bf16)


def dot(a, b):
    return jnp.dot(a, b, preferred_element_type=f32)


def dot_nt(a, b):
    return lax.dot_general(a, b, (((1,), (1,)), ((), ())), preferred_element_type=f32)


def hops(delta, size):
    return min(delta, size - delta)


PLANE_PEERS = sorted(
    ((dx, dy) for dx in range(NX) for dy in range(NY) if dx or dy),
    key=lambda d: -(hops(d[0], NX) + hops(d[1], NY)),
)
Z_PEERS = sorted(range(1, NZ), key=lambda d: -hops(d, NZ))


def body(
    feat_hbm, pos_hbm, wave_hbm, wv_hbm, filt_hbm, gain_hbm, wh_hbm, bh_hbm, wo_hbm,
    out_ref,
    feat_ref, pos_ref, wave_ref, wv_ref, filt_ref, gain_ref, wh_ref, bh_ref, wo_ref,
    xs_ref, ws_ref, turn_ref, high_ref, low_ref, cur_ref, proj_ref, wvt_ref, wht_ref, wot_ref, bht_ref,
    away_ref, home_ref, cross_ref, plane_ref, mine_ref, depth_ref, fact_ref, acc_ref,
    load_sem,
    cross_send, cross_recv, plane_send, plane_recv, depth_send, depth_recv,
    spread_send, spread_recv, pair_send, pair_recv,
    *, comm,
):
    loads = [
        pltpu.make_async_copy(source, target, load_sem.at[i])
        for i, (source, target) in enumerate(
            (
                (pos_hbm, pos_ref), (wave_hbm, wave_ref), (feat_hbm, feat_ref), (wv_hbm, wv_ref), (gain_hbm, gain_ref),
                (wh_hbm, wh_ref), (bh_hbm, bh_ref), (wo_hbm, wo_ref), (filt_hbm, filt_ref),
            )
        )
    ]
    for copy in loads:
        copy.start()

    outer, atoms = lax.axis_index("outer"), lax.axis_index("atoms")
    core, y = lax.rem(outer, 2), lax.rem(atoms, 2) * 2 + lax.div(outer, 2)
    x, z = lax.rem(lax.div(atoms, 2), NX), lax.div(atoms, 2 * NX)
    me = x * NY + y

    def device(x, y, z, core):
        return (lax.rem(y, 2) * 2 + core, z * (2 * NX) + x * 2 + lax.div(y, 2))

    plane_peers, z_peers = {}, {}
    for delta in PLANE_PEERS:
        px, py = lax.rem(x + delta[0], NX), lax.rem(y + delta[1], NY)
        plane_peers[delta] = (px * NY + py, device(px, py, z, core))
    for delta in Z_PEERS:
        z_peers[delta] = device(x, y, lax.rem(z + delta, NZ), core)

    def plane_peer(delta):
        return plane_peers[delta]

    other_core = device(x, y, z, 1 - core)

    def z_peer(delta):
        return z_peers[delta]

    def send(source, target, send_sem, recv_sem, to):
        if comm:
            pltpu.make_async_remote_copy(
                src_ref=source, dst_ref=target, send_sem=send_sem, recv_sem=recv_sem,
                device_id=to, device_id_type=MESH,
            ).start()

    def wait(like, sem):
        if comm:
            pltpu.make_async_copy(like, like, sem).wait()

    if comm:
        barrier = pltpu.get_barrier_semaphore()
        for delta in PLANE_PEERS:
            pl.semaphore_signal(barrier, 1, device_id=plane_peer(delta)[1], device_id_type=MESH)
        for delta in Z_PEERS:
            pl.semaphore_signal(barrier, 1, device_id=z_peer(delta), device_id_type=MESH)
        pl.semaphore_signal(barrier, 1, device_id=other_core, device_id_type=MESH)

    for copy in loads[:2]:
        copy.wait()
    positions = pos_ref[...]
    waves = wave_ref[...].astype(f32)
    xs_ref[...] = jnp.zeros_like(xs_ref)
    ws_ref[...] = jnp.zeros_like(ws_ref)
    for i in range(3):
        xs_ref[3 * i : 3 * i + 3, :] = ((positions >> (8 * i)) & 255).astype(f32)
        ws_ref[3 * i : 3 * i + 3, :] = waves * (256.0**i / TURN)
    turn_ref[...] = dot(ws_ref[...].T.astype(bf16), xs_ref[...].astype(bf16))

    def transposed(matrix, held, b):
        high, low = split(matrix.T)
        held[b] = jnp.concatenate([high, high, low], axis=1)

    def weighted(held, b, value):
        high, low = split(value)
        return dot(held[b], jnp.concatenate([high, low, high], axis=0))

    def project(b):
        high, low = split(weighted(wvt_ref, b, cur_ref[...]).T)
        proj_ref[:, :CHANNELS] = high
        proj_ref[:, CHANNELS:] = low

    def chunk_rows(chunk):
        return pl.ds(pl.multiple_of(chunk * CHUNK, CHUNK), CHUNK)

    def table(chunk):
        table_rows(chunk, 0, CHUNK)

    def table_rows(chunk, i, group):
        for j in range(group // 16):
            octet = chunk * (CHUNK // 16) + i * (group // 16) + j
            t = turn_ref[pl.ds(pl.multiple_of(octet * 8, 8), 8), :]
            r = t - jnp.round(t)
            u = r * r
            s = horner(SIN, u) * r
            high, low = split(jnp.concatenate([1.0 - s * s, s * horner(COS, u)], axis=0))
            at = pl.ds(pl.multiple_of(octet * 16, 16), 16)
            high_ref[at, :] = high
            low_ref[at, :] = low

    def factor(rows):
        a = dot(high_ref[rows, :], proj_ref[...])
        b = dot(low_ref[rows, :], proj_ref[:, :CHANNELS])
        return (a[:, :CHANNELS] + a[:, CHANNELS:]) + b

    def hand_over(b, q):
        send(away_ref.at[b, q], cross_ref.at[b, q], cross_send.at[b, q], cross_recv.at[b, q], other_core)

    def reduce_plane(b, q):
        wait(cross_ref.at[b, q], cross_recv.at[b, q])
        home_ref[b, q] += cross_ref[b, q]
        for delta in PLANE_PEERS:
            peer, to = plane_peer(delta)
            send(
                home_ref.at[b, q, pl.ds(pl.multiple_of(peer * PIECE, 8), PIECE)],
                plane_ref.at[b, q, me], plane_send.at[b, q], plane_recv.at[b, q], to,
            )
        plane_ref[b, q, me] = home_ref[b, q, pl.ds(pl.multiple_of(me * PIECE, 8), PIECE)]

    table((1 - core) * CHUNKS)
    for copy in loads[2:4]:
        copy.wait()
    high, low = split(feat_ref[...])
    weights = jnp.concatenate(split(wv_ref[0]), axis=1)
    both = dot(high, weights)
    high, low = split(both[:, :CHANNELS] + both[:, CHANNELS:] + dot(low, weights[:, :CHANNELS]))
    proj_ref[:, :CHANNELS] = high
    proj_ref[:, CHANNELS:] = low
    for b in range(BLOCKS):
        order = [(1 - core) * CHUNKS + q for q in range(CHUNKS)] + [core * CHUNKS + q for q in range(CHUNKS)]
        for k, chunk in enumerate(order):
            q = k % CHUNKS
            part_ref = away_ref.at[b, q] if k < CHUNKS else home_ref.at[b, q]
            if b == 0 and k + 1 < len(order):

                def step(i, _, chunk=chunk, part_ref=part_ref, following=order[k + 1]):
                    rows = pl.ds(pl.multiple_of(chunk * CHUNK + i * FUSED, FUSED), FUSED)
                    part = factor(rows)
                    table_rows(following, i, FUSED)
                    part_ref[pl.ds(pl.multiple_of(i * FUSED, FUSED), FUSED), :] = part
                    return 0

                lax.fori_loop(0, CHUNK // FUSED, step, 0)
            else:
                part_ref[...] = factor(chunk_rows(chunk))
            if b:
                ready = [k]
            elif k < CHUNKS - 1:
                ready = []
            elif k == CHUNKS - 1:
                if comm:
                    pl.semaphore_wait(barrier, len(PLANE_PEERS) + len(Z_PEERS) + 1)
                ready = list(range(CHUNKS))
            else:
                ready = [k]
            for j in ready:
                if j < CHUNKS:
                    hand_over(b, j)
                else:
                    reduce_plane(b, j - CHUNKS)
        if b == 0:
            for copy in loads[4:]:
                copy.wait()
            cur_ref[...] = feat_ref[...].T
            for i in range(BLOCKS):
                if i:
                    transposed(wv_ref[i], wvt_ref, i)
                transposed(wh_ref[i] * gain_ref[i : i + 1, :].T, wht_ref, i)
                transposed(wo_ref[i], wot_ref, i)
                bht_ref[i] = jnp.broadcast_to(bh_ref[i : i + 1, :], (CHANNELS, CHANNELS)).T
        for q in range(CHUNKS):
            wait(plane_ref.at[b, q, pl.ds(0, PLANE - 1)], plane_recv.at[b, q])
            mine_ref[b, q] = jnp.sum(plane_ref[b, q], axis=0)
            for delta in Z_PEERS:
                send(mine_ref.at[b, q], depth_ref.at[b, q, z], depth_send.at[b, q], depth_recv.at[b, q], z_peer(delta))
            depth_ref[b, q, z] = mine_ref[b, q]
        for q in range(CHUNKS):
            wait(depth_ref.at[b, q, pl.ds(0, NZ - 1)], depth_recv.at[b, q])
            total = jnp.sum(depth_ref[b, q], axis=0)
            first = (core * CHUNKS + q) * CHUNK + me * PIECE
            parts = []
            for i in range(PIECE // 8):
                octet = (first // 8 + i) // 2
                parts.append(filt_ref[b, pl.ds(pl.multiple_of(octet * 8, 8), 8), :])
            here = fact_ref.at[b, pl.ds(pl.multiple_of(first, 8), PIECE)]
            here[...] = total * jnp.concatenate(parts, axis=0)
            for delta in PLANE_PEERS:
                send(here, here, spread_send.at[b, q], spread_recv.at[b, q], plane_peer(delta)[1])
        for q in range(CHUNKS):
            chunk = pl.ds(pl.multiple_of((core * CHUNKS + q) * CHUNK, CHUNK), CHUNK)
            wait(fact_ref.at[b, pl.ds(0, (PLANE - 1) * PIECE)], spread_recv.at[b, q])
            whole = fact_ref.at[b, chunk]
            send(whole, whole, pair_send.at[b, q], pair_recv.at[b, q], other_core)
        def message(rows):
            high, low = split(fact_ref[b, rows, :].T)
            both = dot(jnp.concatenate([high, low], axis=0), high_ref[rows, :])
            return both[:CHANNELS] + both[CHANNELS:] + dot(high, low_ref[rows, :])

        acc_ref[...] = message(pl.ds(pl.multiple_of(core * HALF, HALF), HALF))
        for first, last in TAIL:
            for q in range(first, last):
                wait(fact_ref.at[b, pl.ds(0, CHUNK)], pair_recv.at[b, q])
            acc_ref[...] += message(pl.ds(pl.multiple_of((1 - core) * HALF + first * CHUNK, 128), (last - first) * CHUNK))
        messages = acc_ref[...]
        scale = lax.rsqrt(jnp.mean(messages * messages, axis=0, keepdims=True) + 1e-6)
        bias = jnp.concatenate([bht_ref[b]] * (ATOMS // CHANNELS), axis=1)
        v = weighted(wht_ref, b, messages) * scale + bias
        hidden = v / (1.0 + jnp.exp(-v))
        cur_ref[...] += weighted(wot_ref, b, hidden)
        if b + 1 < BLOCKS:
            project(b + 1)
    out_ref[...] = cur_ref[...].T
    for b in range(BLOCKS):
        for q in range(CHUNKS):
            wait(away_ref.at[b, q], cross_send.at[b, q])
            wait(plane_ref.at[b, q, pl.ds(0, PLANE - 1)], plane_send.at[b, q])
            wait(depth_ref.at[b, q, pl.ds(0, NZ - 1)], depth_send.at[b, q])
            wait(fact_ref.at[b, pl.ds(0, (PLANE - 1) * PIECE)], spread_send.at[b, q])
            wait(fact_ref.at[b, pl.ds(0, CHUNK)], pair_send.at[b, q])


def local(*operands, comm=True):
    sems = [pltpu.SemaphoreType.DMA((BLOCKS, CHUNKS))] * 10
    return pl.pallas_call(
        functools.partial(body, comm=comm),
        name="ewald",
        out_shape=pltpu.VMEM((ATOMS, CHANNELS), f32),
        in_specs=[pl.BlockSpec(memory_space=pltpu.HBM)] * len(operands),
        out_specs=pl.BlockSpec(memory_space=pltpu.VMEM),
        scratch_shapes=[
            *[pltpu.VMEM(operand.shape, operand.dtype) for operand in operands],
            pltpu.VMEM((16, ATOMS), f32),
            pltpu.VMEM((16, WAVES), f32),
            pltpu.VMEM((WAVES, ATOMS), f32),
            pltpu.VMEM((ROWS, ATOMS), bf16),
            pltpu.VMEM((ROWS, ATOMS), bf16),
            pltpu.VMEM((CHANNELS, ATOMS), f32),
            pltpu.VMEM((ATOMS, 2 * CHANNELS), bf16),
            pltpu.VMEM((BLOCKS, CHANNELS, 3 * CHANNELS), bf16),
            pltpu.VMEM((BLOCKS, CHANNELS, 3 * CHANNELS), bf16),
            pltpu.VMEM((BLOCKS, CHANNELS, 3 * CHANNELS), bf16),
            pltpu.VMEM((BLOCKS, CHANNELS, CHANNELS), f32),
            pltpu.VMEM((BLOCKS, CHUNKS, CHUNK, CHANNELS), f32),
            pltpu.VMEM((BLOCKS, CHUNKS, CHUNK, CHANNELS), f32),
            pltpu.VMEM((BLOCKS, CHUNKS, CHUNK, CHANNELS), f32),
            pltpu.VMEM((BLOCKS, CHUNKS, PLANE, PIECE, CHANNELS), f32),
            pltpu.VMEM((BLOCKS, CHUNKS, PIECE, CHANNELS), f32),
            pltpu.VMEM((BLOCKS, CHUNKS, NZ, PIECE, CHANNELS), f32),
            pltpu.VMEM((BLOCKS, ROWS, CHANNELS), f32),
            pltpu.VMEM((CHANNELS, ATOMS), f32),
            pltpu.SemaphoreType.DMA((9,)),
            *sems,
        ],
        compiler_params=pltpu.CompilerParams(
            collective_id=0 if comm else None,
            has_side_effects=True,
            vmem_limit_bytes=56 << 20,
        ),
    )(*operands)


def solution(mesh):
    rows = P(("outer", "atoms"), None)
    return jax.shard_map(
        local,
        mesh=mesh,
        in_specs=(rows, P(None, ("outer", "atoms")), *[P()] * 7),
        out_specs=rows,
        check_vma=False,
    )
```

```python
import functools

import jax
import jax.numpy as jnp
from jax import lax
from jax.experimental import pallas as pl
from jax.experimental.pallas import tpu as pltpu
from jax.sharding import PartitionSpec as P

MESH = pl.DeviceIdType.MESH
f32 = jnp.float32
bf16 = jnp.bfloat16

NX, NY, NZ = 4, 4, 8
PLANE = NX * NY
ATOMS, CHANNELS, WAVES, BLOCKS = 1024, 128, 768, 2
ROWS = 2 * WAVES
HALF = ROWS // 2
CHUNKS = 3
CHUNK = HALF // CHUNKS
PIECE = CHUNK // PLANE
TURN = 262144.0
FUSED = 256
TAIL = ((0, CHUNKS - 1), (CHUNKS - 1, CHUNKS))

SIN = (4.442882834149947, -7.308241154547219, 3.6062889582380353, -0.8457635962127477, 0.10920575375428615)
COS = (1.4142134965650266, -6.978850988240709, 5.739461170716688, -1.8835629875263915, 0.31069819226115863)


def horner(coefficients, u):
    total = jnp.full_like(u, coefficients[-1])
    for c in coefficients[-2::-1]:
        total = total * u + c
    return total


def split(value):
    high = value.astype(bf16)
    return high, (value - high.astype(f32)).astype(bf16)


def dot(a, b):
    return jnp.dot(a, b, preferred_element_type=f32)


def dot_nt(a, b):
    return lax.dot_general(a, b, (((1,), (1,)), ((), ())), preferred_element_type=f32)


def hops(delta, size):
    return min(delta, size - delta)


PLANE_PEERS = sorted(
    ((dx, dy) for dx in range(NX) for dy in range(NY) if dx or dy),
    key=lambda d: -(hops(d[0], NX) + hops(d[1], NY)),
)
Z_PEERS = sorted(range(1, NZ), key=lambda d: -hops(d, NZ))


def body(
    feat_hbm, pos_hbm, wave_hbm, wv_hbm, filt_hbm, gain_hbm, wh_hbm, bh_hbm, wo_hbm,
    out_ref,
    feat_ref, pos_ref, wave_ref, wv_ref, filt_ref, gain_ref, wh_ref, bh_ref, wo_ref,
    xs_ref, ws_ref, turn_ref, high_ref, low_ref, cur_ref, proj_ref, wvt_ref, wht_ref, wot_ref, bht_ref,
    away_ref, home_ref, cross_ref, plane_ref, mine_ref, depth_ref, fact_ref, acc_ref,
    load_sem,
    cross_send, cross_recv, plane_send, plane_recv, depth_send, depth_recv,
    spread_send, spread_recv, pair_send, pair_recv,
    *, comm,
):
    loads = [
        pltpu.make_async_copy(source, target, load_sem.at[i])
        for i, (source, target) in enumerate(
            (
                (pos_hbm, pos_ref), (wave_hbm, wave_ref), (feat_hbm, feat_ref), (wv_hbm, wv_ref), (gain_hbm, gain_ref),
                (wh_hbm, wh_ref), (bh_hbm, bh_ref), (wo_hbm, wo_ref), (filt_hbm, filt_ref),
            )
        )
    ]
    for copy in loads:
        copy.start()

    outer, atoms = lax.axis_index("outer"), lax.axis_index("atoms")
    core, y = lax.rem(outer, 2), lax.rem(atoms, 2) * 2 + lax.div(outer, 2)
    x, z = lax.rem(lax.div(atoms, 2), NX), lax.div(atoms, 2 * NX)
    me = x * NY + y

    def device(x, y, z, core):
        return (lax.rem(y, 2) * 2 + core, z * (2 * NX) + x * 2 + lax.div(y, 2))

    plane_peers, z_peers = {}, {}
    for delta in PLANE_PEERS:
        px, py = lax.rem(x + delta[0], NX), lax.rem(y + delta[1], NY)
        plane_peers[delta] = (px * NY + py, device(px, py, z, core))
    for delta in Z_PEERS:
        z_peers[delta] = device(x, y, lax.rem(z + delta, NZ), core)

    def plane_peer(delta):
        return plane_peers[delta]

    other_core = device(x, y, z, 1 - core)

    def z_peer(delta):
        return z_peers[delta]

    def send(source, target, send_sem, recv_sem, to):
        if comm:
            pltpu.make_async_remote_copy(
                src_ref=source, dst_ref=target, send_sem=send_sem, recv_sem=recv_sem,
                device_id=to, device_id_type=MESH,
            ).start()

    def wait(like, sem):
        if comm:
            pltpu.make_async_copy(like, like, sem).wait()

    if comm:
        barrier = pltpu.get_barrier_semaphore()
        for delta in PLANE_PEERS:
            pl.semaphore_signal(barrier, 1, device_id=plane_peer(delta)[1], device_id_type=MESH)
        for delta in Z_PEERS:
            pl.semaphore_signal(barrier, 1, device_id=z_peer(delta), device_id_type=MESH)
        pl.semaphore_signal(barrier, 1, device_id=other_core, device_id_type=MESH)

    for copy in loads[:2]:
        copy.wait()
    positions = pos_ref[...]
    waves = wave_ref[...].astype(f32)
    xs_ref[...] = jnp.zeros_like(xs_ref)
    ws_ref[...] = jnp.zeros_like(ws_ref)
    for i in range(3):
        xs_ref[3 * i : 3 * i + 3, :] = ((positions >> (8 * i)) & 255).astype(f32)
        ws_ref[3 * i : 3 * i + 3, :] = waves * (256.0**i / TURN)
    turn_ref[...] = dot(ws_ref[...].T.astype(bf16), xs_ref[...].astype(bf16))

    def transposed(matrix, held, b):
        high, low = split(matrix.T)
        held[b] = jnp.concatenate([high, high, low], axis=1)

    def weighted(held, b, value):
        high, low = split(value)
        return dot(held[b], jnp.concatenate([high, low, high], axis=0))

    def project(b):
        high, low = split(weighted(wvt_ref, b, cur_ref[...]).T)
        proj_ref[:, :CHANNELS] = high
        proj_ref[:, CHANNELS:] = low

    def chunk_rows(chunk):
        return pl.ds(pl.multiple_of(chunk * CHUNK, CHUNK), CHUNK)

    def table(chunk):
        table_rows(chunk, 0, CHUNK)

    def table_rows(chunk, i, group):
        for j in range(group // 16):
            octet = chunk * (CHUNK // 16) + i * (group // 16) + j
            t = turn_ref[pl.ds(pl.multiple_of(octet * 8, 8), 8), :]
            r = t - jnp.round(t)
            u = r * r
            s = horner(SIN, u) * r
            high, low = split(jnp.concatenate([1.0 - s * s, s * horner(COS, u)], axis=0))
            at = pl.ds(pl.multiple_of(octet * 16, 16), 16)
            high_ref[at, :] = high
            low_ref[at, :] = low

    def factor(rows):
        a = dot(high_ref[rows, :], proj_ref[...])
        b = dot(low_ref[rows, :], proj_ref[:, :CHANNELS])
        return (a[:, :CHANNELS] + a[:, CHANNELS:]) + b

    def hand_over(b, q):
        send(away_ref.at[b, q], cross_ref.at[b, q], cross_send.at[b, q], cross_recv.at[b, q], other_core)

    def reduce_plane(b, q):
        wait(cross_ref.at[b, q], cross_recv.at[b, q])
        home_ref[b, q] += cross_ref[b, q]
        for delta in PLANE_PEERS:
            peer, to = plane_peer(delta)
            send(
                home_ref.at[b, q, pl.ds(pl.multiple_of(peer * PIECE, 8), PIECE)],
                plane_ref.at[b, q, me], plane_send.at[b, q], plane_recv.at[b, q], to,
            )
        plane_ref[b, q, me] = home_ref[b, q, pl.ds(pl.multiple_of(me * PIECE, 8), PIECE)]

    table((1 - core) * CHUNKS)
    for copy in loads[2:4]:
        copy.wait()
    high, low = split(feat_ref[...])
    weights = jnp.concatenate(split(wv_ref[0]), axis=1)
    both = dot(high, weights)
    high, low = split(both[:, :CHANNELS] + both[:, CHANNELS:] + dot(low, weights[:, :CHANNELS]))
    proj_ref[:, :CHANNELS] = high
    proj_ref[:, CHANNELS:] = low
    for b in range(BLOCKS):
        order = [(1 - core) * CHUNKS + q for q in range(CHUNKS)] + [core * CHUNKS + q for q in range(CHUNKS)]
        for k, chunk in enumerate(order):
            q = k % CHUNKS
            part_ref = away_ref.at[b, q] if k < CHUNKS else home_ref.at[b, q]
            if b == 0 and k + 1 < len(order):

                def step(i, _, chunk=chunk, part_ref=part_ref, following=order[k + 1]):
                    rows = pl.ds(pl.multiple_of(chunk * CHUNK + i * FUSED, FUSED), FUSED)
                    part = factor(rows)
                    table_rows(following, i, FUSED)
                    part_ref[pl.ds(pl.multiple_of(i * FUSED, FUSED), FUSED), :] = part
                    return 0

                lax.fori_loop(0, CHUNK // FUSED, step, 0)
            else:
                part_ref[...] = factor(chunk_rows(chunk))
            if b:
                ready = [k]
            elif k < CHUNKS - 2:
                ready = []
            elif k == CHUNKS - 2:
                if comm:
                    pl.semaphore_wait(barrier, len(PLANE_PEERS) + len(Z_PEERS) + 1)
                ready = list(range(CHUNKS - 1))
            else:
                ready = [k]
            for j in ready:
                if j < CHUNKS:
                    hand_over(b, j)
                else:
                    reduce_plane(b, j - CHUNKS)
        if b == 0:
            for copy in loads[4:]:
                copy.wait()
            cur_ref[...] = feat_ref[...].T
            for i in range(BLOCKS):
                if i:
                    transposed(wv_ref[i], wvt_ref, i)
                transposed(wh_ref[i] * gain_ref[i : i + 1, :].T, wht_ref, i)
                transposed(wo_ref[i], wot_ref, i)
                bht_ref[i] = jnp.broadcast_to(bh_ref[i : i + 1, :], (CHANNELS, CHANNELS)).T
        for q in range(CHUNKS):
            wait(plane_ref.at[b, q, pl.ds(0, PLANE - 1)], plane_recv.at[b, q])
            mine_ref[b, q] = jnp.sum(plane_ref[b, q], axis=0)
            for delta in Z_PEERS:
                send(mine_ref.at[b, q], depth_ref.at[b, q, z], depth_send.at[b, q], depth_recv.at[b, q], z_peer(delta))
            depth_ref[b, q, z] = mine_ref[b, q]
        for q in range(CHUNKS):
            wait(depth_ref.at[b, q, pl.ds(0, NZ - 1)], depth_recv.at[b, q])
            total = jnp.sum(depth_ref[b, q], axis=0)
            first = (core * CHUNKS + q) * CHUNK + me * PIECE
            parts = []
            for i in range(PIECE // 8):
                octet = (first // 8 + i) // 2
                parts.append(filt_ref[b, pl.ds(pl.multiple_of(octet * 8, 8), 8), :])
            here = fact_ref.at[b, pl.ds(pl.multiple_of(first, 8), PIECE)]
            here[...] = total * jnp.concatenate(parts, axis=0)
            for delta in PLANE_PEERS:
                send(here, here, spread_send.at[b, q], spread_recv.at[b, q], plane_peer(delta)[1])
        for q in range(CHUNKS):
            chunk = pl.ds(pl.multiple_of((core * CHUNKS + q) * CHUNK, CHUNK), CHUNK)
            wait(fact_ref.at[b, pl.ds(0, (PLANE - 1) * PIECE)], spread_recv.at[b, q])
            whole = fact_ref.at[b, chunk]
            send(whole, whole, pair_send.at[b, q], pair_recv.at[b, q], other_core)
        def message(rows):
            high, low = split(fact_ref[b, rows, :].T)
            both = dot(jnp.concatenate([high, low], axis=0), high_ref[rows, :])
            return both[:CHANNELS] + both[CHANNELS:] + dot(high, low_ref[rows, :])

        acc_ref[...] = message(pl.ds(pl.multiple_of(core * HALF, HALF), HALF))
        for first, last in TAIL:
            for q in range(first, last):
                wait(fact_ref.at[b, pl.ds(0, CHUNK)], pair_recv.at[b, q])
            acc_ref[...] += message(pl.ds(pl.multiple_of((1 - core) * HALF + first * CHUNK, 128), (last - first) * CHUNK))
        messages = acc_ref[...]
        scale = lax.rsqrt(jnp.mean(messages * messages, axis=0, keepdims=True) + 1e-6)
        bias = jnp.concatenate([bht_ref[b]] * (ATOMS // CHANNELS), axis=1)
        v = weighted(wht_ref, b, messages) * scale + bias
        hidden = v / (1.0 + jnp.exp(-v))
        cur_ref[...] += weighted(wot_ref, b, hidden)
        if b + 1 < BLOCKS:
            project(b + 1)
    out_ref[...] = cur_ref[...].T
    for b in range(BLOCKS):
        for q in range(CHUNKS):
            wait(away_ref.at[b, q], cross_send.at[b, q])
            wait(plane_ref.at[b, q, pl.ds(0, PLANE - 1)], plane_send.at[b, q])
            wait(depth_ref.at[b, q, pl.ds(0, NZ - 1)], depth_send.at[b, q])
            wait(fact_ref.at[b, pl.ds(0, (PLANE - 1) * PIECE)], spread_send.at[b, q])
            wait(fact_ref.at[b, pl.ds(0, CHUNK)], pair_send.at[b, q])


def local(*operands, comm=True):
    sems = [pltpu.SemaphoreType.DMA((BLOCKS, CHUNKS))] * 10
    return pl.pallas_call(
        functools.partial(body, comm=comm),
        name="ewald",
        out_shape=pltpu.VMEM((ATOMS, CHANNELS), f32),
        in_specs=[pl.BlockSpec(memory_space=pltpu.HBM)] * len(operands),
        out_specs=pl.BlockSpec(memory_space=pltpu.VMEM),
        scratch_shapes=[
            *[pltpu.VMEM(operand.shape, operand.dtype) for operand in operands],
            pltpu.VMEM((16, ATOMS), f32),
            pltpu.VMEM((16, WAVES), f32),
            pltpu.VMEM((WAVES, ATOMS), f32),
            pltpu.VMEM((ROWS, ATOMS), bf16),
            pltpu.VMEM((ROWS, ATOMS), bf16),
            pltpu.VMEM((CHANNELS, ATOMS), f32),
            pltpu.VMEM((ATOMS, 2 * CHANNELS), bf16),
            pltpu.VMEM((BLOCKS, CHANNELS, 3 * CHANNELS), bf16),
            pltpu.VMEM((BLOCKS, CHANNELS, 3 * CHANNELS), bf16),
            pltpu.VMEM((BLOCKS, CHANNELS, 3 * CHANNELS), bf16),
            pltpu.VMEM((BLOCKS, CHANNELS, CHANNELS), f32),
            pltpu.VMEM((BLOCKS, CHUNKS, CHUNK, CHANNELS), f32),
            pltpu.VMEM((BLOCKS, CHUNKS, CHUNK, CHANNELS), f32),
            pltpu.VMEM((BLOCKS, CHUNKS, CHUNK, CHANNELS), f32),
            pltpu.VMEM((BLOCKS, CHUNKS, PLANE, PIECE, CHANNELS), f32),
            pltpu.VMEM((BLOCKS, CHUNKS, PIECE, CHANNELS), f32),
            pltpu.VMEM((BLOCKS, CHUNKS, NZ, PIECE, CHANNELS), f32),
            pltpu.VMEM((BLOCKS, ROWS, CHANNELS), f32),
            pltpu.VMEM((CHANNELS, ATOMS), f32),
            pltpu.SemaphoreType.DMA((9,)),
            *sems,
        ],
        compiler_params=pltpu.CompilerParams(
            collective_id=0 if comm else None,
            has_side_effects=True,
            vmem_limit_bytes=56 << 20,
        ),
    )(*operands)


def solution(mesh):
    rows = P(("outer", "atoms"), None)
    return jax.shard_map(
        local,
        mesh=mesh,
        in_specs=(rows, P(None, ("outer", "atoms")), *[P()] * 7),
        out_specs=rows,
        check_vma=False,
    )
```
